32 devices in a mesh: groups: 2 (over x), context: 16 (over z, y, core).
Axes of the slice: x: 2, y: 2, z: 4, core: 2. Of those that a mesh axis runs over, the one named last changes fastest.
Arguments:
- projected: bfloat16 [4096, 3072], P(('groups', 'context')), parts along dimension 0, may hold values from -6 to 6
- short_filter: bfloat16 [3, 3072], replicated, may hold values from -3.5 to 3.5
- filter_taps: float32 [2048, 64], P('context'), may hold values from -2 to 2
- bank: int32 [1024], replicated, may hold values from 0 to 63
- skip: float32 [1024], replicated, may hold values from -1 to 1
Outputs:
- gated_output: bfloat16 [4096, 1024], P(('groups', 'context')), parts along dimension 0
The draws below stay inside these ranges and needn't reach their ends.
There are 2 independent parts, one for each index of `groups`. The reference program is written for one: setup_inputs(seed, part) draws one part's arguments, and reference() takes and returns one part's arrays. A program takes and returns all parts, laid end to end along the dimension named above; an argument that names none is the same for every part. Nothing has to cross between parts.
All inputs are finite; a program needn't handle non-finite values.
Results may differ from the reference program's by a relative error of at most 0.001.
Values may be sent and summed in bfloat16 or wider, within the bound.
A program may use at most 64 MiB of HBM per device.

```python
import jax
import jax.numpy as jnp

CH = 1024
FB = 64
SEQ = 2048


def draw_filter_taps(key, part):
    key = jax.random.fold_in(key, 7)
    first_key, second_key = jax.random.split(key, 2)
    times = jnp.arange(SEQ, dtype=jnp.float32)[:, None]
    exponent = jax.random.uniform(first_key, (FB,), jnp.float32, 0.0, 1.0)
    noise = jnp.clip(jax.random.normal(second_key, (SEQ, FB), jnp.float32), -3.0, 3.0)
    decay_length = 8.0 * (SEQ / 8.0) ** exponent
    envelope = jnp.exp(-times / decay_length[None, :])
    amplitude = 0.7 * jnp.sqrt(2.0 / decay_length)
    return (noise * envelope * amplitude[None, :]).astype(jnp.float32)


def plant(values, own_key, least, largest):
    dims = values.shape
    index_at = [jax.random.randint(jax.random.fold_in(own_key, axis), (), 0, dims[axis]) for axis in range(len(dims))]
    values = values.at[tuple(index_at)].set(least)
    longest = dims.index(max(dims))
    index_at[longest] = (index_at[longest] + 1) % dims[longest]
    return values.at[tuple(index_at)].set(largest)


def steps_of(stream_key, dims, cuts, low, largest):
    level = 1.0
    for position, blocks in cuts:
        draws = jax.random.uniform(jax.random.fold_in(jax.random.fold_in(stream_key, 6), position), (blocks,), jnp.float32, low / len(cuts), largest / len(cuts))
        level = level * jnp.repeat(jnp.exp(draws), dims[position] // blocks).reshape((-1,) + (1,) * (len(dims) - 1 - position))
    return level


def centred(key, dims, spread, reach, cuts=(), kind=jnp.bfloat16):
    values = jax.random.normal(key, dims, jnp.float32) * spread
    if len(cuts) > 0:
        values = steps_of(key, dims, cuts, -0.22, 0.18) * values
    return jnp.clip(values, min=-reach, max=reach).astype(kind)


def setup_inputs(seed: int = 0, part: int = 0) -> dict:
    splits = jax.random.split(jax.random.key(seed), 6)
    part_splits = jax.random.split(jax.random.fold_in(splits[5], part), 6)
    projected = centred(part_splits[0], (SEQ, 3 * CH), 1.0, 6.0, ((0, 16),))
    short_filter = centred(splits[1], (3, 3 * CH), 3 ** -0.5, 3.5)
    filter_taps = draw_filter_taps(jax.random.fold_in(splits[5], 71), part)
    bank = plant(jax.random.randint(splits[3], (CH,), 0, FB), jax.random.fold_in(splits[3], 1), 0, FB - 1).astype(jnp.int32)
    skip = jnp.clip(jax.random.uniform(splits[4], (CH,), jnp.float32, -1.0, 1.0), -1.0, 1.0)
    return dict(projected=projected, short_filter=short_filter, filter_taps=filter_taps, bank=bank, skip=skip)


def reference(projected, short_filter, filter_taps, bank, skip):
    inputs = projected.astype(jnp.float32)
    weights = short_filter.astype(jnp.float32)
    padded = jnp.concatenate([jnp.zeros((2, inputs.shape[1]), jnp.float32), inputs], axis=0)
    featured = weights[0] * padded[2:] + weights[1] * padded[1:-1] + weights[2] * padded[:-2]
    query = featured[:, :CH]
    key_part = featured[:, CH:2 * CH]
    value_part = featured[:, 2 * CH:]
    mixed = key_part * value_part
    taps = jnp.take(filter_taps, bank, axis=1)
    spectrum = jnp.fft.rfft(mixed, n=2 * SEQ, axis=0) * jnp.fft.rfft(taps, n=2 * SEQ, axis=0)
    convolved = jnp.fft.irfft(spectrum, n=2 * SEQ, axis=0)[:SEQ]
    return (query * (convolved + skip * mixed)).astype(jnp.bfloat16)
```

```python
import functools
import math

import jax
import jax.numpy as jnp
import ml_dtypes
import numpy as np
from jax import lax
from jax.experimental import pallas as pl
from jax.experimental.pallas import tpu as pltpu
from jax.sharding import PartitionSpec as P

HIGHEST = lax.Precision.HIGHEST


def from_partner(array, axis, distance):
    return lax.ppermute(array, axis, [(i, i ^ 1 << distance) for i in range(lax.axis_size(axis))])


def from_behind(array, axis, by):
    count = lax.axis_size(axis)
    pairs = [(i, i + by) for i in range(count) if 0 <= i + by < count]
    return lax.ppermute(array, axis, pairs)


def phases(numer, period, sign):
    angle = sign * 2.0 * math.pi / period * (numer % period).astype(jnp.float32)
    return (jnp.cos(angle), jnp.sin(angle))


def local_table(length, sign):
    places = jnp.arange(length, dtype=jnp.int32)
    return phases(places[:, None] * places[None, :], length, sign)


def rotate(real, imag, cosine, sine):
    return (real * cosine - imag * sine, real * sine + imag * cosine)


def complex_product(left_real, left_imag, right_real, right_imag):
    out_real = jnp.dot(left_real, right_real, precision=HIGHEST) - jnp.dot(
        left_imag, right_imag, precision=HIGHEST
    )
    out_imag = jnp.dot(left_real, right_imag, precision=HIGHEST) + jnp.dot(
        left_imag, right_real, precision=HIGHEST
    )
    return (out_real, out_imag)


def forward_transform(real, imag, length_total, shards, my_index):
    levels = shards.bit_length() - 1
    steps = real.shape[0]
    for level in range(levels - 1, -1, -1):
        span = 1 << level
        other_real, other_imag = from_partner((real, imag), "context", level)
        upper = my_index >> level & 1 == 1
        cosine, sine = phases(my_index % span, 2 * span, -1.0)
        turned_real, turned_imag = rotate(other_real - real, other_imag - imag, cosine, sine)
        real = jnp.where(upper, turned_real, real + other_real)
        imag = jnp.where(upper, turned_imag, imag + other_imag)
    frequency = jnp.zeros((), jnp.int32)
    for level in range(levels):
        frequency = frequency | (my_index >> level & 1) << levels - 1 - level
    position = jnp.arange(steps, dtype=jnp.int32)
    cosine, sine = phases(position * frequency, length_total, -1.0)
    real, imag = rotate(real, imag, cosine[:, None], sine[:, None])
    table_cos, table_sin = local_table(steps, -1.0)
    real, imag = complex_product(table_cos, table_sin, real, imag)
    return (real, imag, frequency)


def inverse_transform(real, imag, frequency, length_total, shards, my_index):
    levels = shards.bit_length() - 1
    steps = real.shape[0]
    table_cos, table_sin = local_table(steps, 1.0)
    real, imag = complex_product(table_cos / steps, table_sin / steps, real, imag)
    position = jnp.arange(steps, dtype=jnp.int32)
    cosine, sine = phases(position * frequency, length_total, 1.0)
    real, imag = rotate(real, imag, cosine[:, None], sine[:, None])
    for level in range(levels):
        span = 1 << level
        other_real, other_imag = from_partner((real, imag), "context", level)
        upper = my_index >> level & 1 == 1
        cosine, sine = phases(my_index % span, 2 * span, 1.0)
        mine_real, mine_imag = rotate(real, imag, cosine, sine)
        theirs_real, theirs_imag = rotate(other_real, other_imag, cosine, sine)
        real_next = jnp.where(upper, 0.5 * (other_real - mine_real), 0.5 * (real + theirs_real))
        imag_next = jnp.where(upper, 0.5 * (other_imag - mine_imag), 0.5 * (imag + theirs_imag))
        real, imag = (real_next, imag_next)
    return (real, imag)


def per_device_spectral(projected, short_filter, filter_taps, bank, skip):
    steps = projected.shape[0]
    shards = lax.axis_size("context")
    my_index = lax.axis_index("context")
    length_total = steps * shards
    channels = skip.shape[0]
    banks = filter_taps.shape[1]
    earlier = from_behind(projected[steps - 2 :], "context", 1)
    joined = jnp.concatenate([earlier, projected], axis=0)
    weights = short_filter.astype(jnp.float32)
    featured = weights[0] * joined[2:] + weights[1] * joined[1:-1] + weights[2] * joined[:-2]
    query = featured[:, :channels]
    key_part = featured[:, channels : 2 * channels]
    value_part = featured[:, 2 * channels :]
    mixed = key_part * value_part
    signal = jnp.concatenate([mixed, filter_taps], axis=1)
    position = my_index * steps + jnp.arange(steps, dtype=jnp.int32)
    cosine, sine = phases(position, 2 * length_total, -1.0)
    real = jnp.concatenate([signal, signal * cosine[:, None]], axis=1)
    imag = jnp.concatenate([jnp.zeros_like(signal), signal * sine[:, None]], axis=1)
    spec_real, spec_imag, frequency = forward_transform(real, imag, length_total, shards, my_index)
    width = channels + banks
    selector = (bank[None, :] == jnp.arange(banks, dtype=jnp.int32)[:, None]).astype(jnp.float32)
    real_parts = []
    imag_parts = []
    for branch in range(2):
        offset = branch * width
        data_real = spec_real[:, offset : offset + channels]
        data_imag = spec_imag[:, offset : offset + channels]
        filter_real = jnp.dot(
            spec_real[:, offset + channels : offset + width], selector, precision=HIGHEST
        )
        filter_imag = jnp.dot(
            spec_imag[:, offset + channels : offset + width], selector, precision=HIGHEST
        )
        real_parts.append(data_real * filter_real - data_imag * filter_imag)
        imag_parts.append(data_real * filter_imag + data_imag * filter_real)
    product_real = jnp.concatenate(real_parts, axis=1)
    product_imag = jnp.concatenate(imag_parts, axis=1)
    back_real, back_imag = inverse_transform(
        product_real, product_imag, frequency, length_total, shards, my_index
    )
    cos_back, sin_back = phases(position, 2 * length_total, 1.0)
    second = (
        back_real[:, channels:] * cos_back[:, None] - back_imag[:, channels:] * sin_back[:, None]
    )
    convolved = 0.5 * (back_real[:, :channels] + second)
    return (query * (convolved + skip * mixed)).astype(jnp.bfloat16)


LANES = 128
F32 = jnp.float32
BF16 = jnp.bfloat16


def split_rows(table):
    high = table.astype(ml_dtypes.bfloat16)
    low = (table - high.astype(np.float64)).astype(ml_dtypes.bfloat16)
    return np.concatenate([high, high, low], axis=1)


def block_tables(steps):
    angle = np.pi / steps * (np.arange(steps)[:, None] + 0.5) * np.arange(steps)[None, :]
    forward = np.concatenate([np.cos(angle), -np.sin(angle)], axis=0)
    inverse = np.concatenate([np.cos(angle.T), -np.sin(angle.T)], axis=1) / steps
    return split_rows(forward), split_rows(inverse)


def stacked(values):
    high = values.astype(BF16)
    low = (values - high.astype(F32)).astype(BF16)
    return jnp.concatenate([high, low, high], axis=0)


def kernel(
    shards,
    projected,
    short_filter,
    taps,
    bank,
    skip,
    forward,
    inverse,
    out,
    halo,
    signal_out,
    signal_in,
    taps_in,
    query,
    direct,
    signal_spec,
    taps_spec,
    pairs,
    result_out,
    result_in,
    halo_sem,
    signal_sent,
    signal_got,
    taps_sent,
    taps_passed,
    taps_got,
    result_sent,
    result_got,
):
    me = lax.axis_index("context")
    steps = projected.shape[0]
    half = steps // 2
    channels = out.shape[1]
    chips = shards // 2
    chip = lax.div(me, 2)
    core = lax.rem(me, 2)
    sibling = me + 1 - 2 * core
    left_lanes = lax.broadcasted_iota(jnp.int32, (half, LANES), 1) < LANES // 2

    def remote(src, dst, sent, got, target):
        return pltpu.make_async_remote_copy(
            src_ref=src,
            dst_ref=dst,
            send_sem=sent,
            recv_sem=got,
            device_id={"context": target},
            device_id_type=pl.DeviceIdType.MESH,
        )

    def arrived(ref, got):
        pltpu.make_async_copy(ref, ref, got).wait()

    def turned(values):
        return pltpu.roll(values, LANES // 2, 1)

    def exchange(first, second):
        return (
            jnp.where(left_lanes, first, turned(second)),
            jnp.where(left_lanes, turned(first), second),
        )

    barrier = pltpu.get_barrier_semaphore()
    for off in range(1, shards):
        pl.semaphore_signal(
            barrier,
            inc=1,
            device_id={"context": lax.rem(me + off, shards)},
            device_id_type=pl.DeviceIdType.MESH,
        )
    values = jnp.concatenate([taps[:half, :], taps[half:, :]], axis=1)
    high = values.astype(BF16)
    taps_in[me] = jnp.concatenate([high, (values - high.astype(F32)).astype(BF16)], axis=0)
    pl.semaphore_wait(barrier, shards - 1)

    behind = remote(
        projected.at[pl.ds(steps - 16, 16)],
        halo,
        halo_sem.at[0],
        halo_sem.at[1],
        lax.rem(me + 1, shards),
    )
    behind.start()

    def taps_copy(off):
        target = lax.rem(me + 2 * off, shards)
        return remote(taps_in.at[me], taps_in.at[me], taps_sent.at[off], taps_got.at[me], target)

    def taps_pass(off):
        slot = lax.rem(me + shards - 2 * off, shards)
        return remote(
            taps_in.at[slot], taps_in.at[slot], taps_passed.at[off], taps_got.at[slot], sibling
        )

    taps_pass(0).start()

    @pl.loop(1, chips)
    def _(off):
        taps_copy(off).start()

    behind.wait()
    row = lax.broadcasted_iota(jnp.int32, (steps, LANES), 0)

    def featured(start):
        columns = pl.ds(pl.multiple_of(start, LANES), LANES)
        values = projected[:, columns].astype(F32)
        earlier = halo[:, columns].astype(F32)
        earlier = jnp.where(me == 0, 0.0, earlier)
        weights = short_filter[:, columns].astype(F32)
        last = earlier[15:16]
        once = jnp.where(row == 0, last, pltpu.roll(values, 1, 0))
        twice = jnp.where(
            row == 0, earlier[14:15], jnp.where(row == 1, last, pltpu.roll(values, 2, 0))
        )
        return weights[0:1] * values + weights[1:2] * once + weights[2:3] * twice

    def signal_copy(target, index):
        return remote(
            signal_out.at[target],
            signal_in.at[me],
            signal_sent.at[index],
            signal_got.at[me],
            target,
        )

    def make_signal(tile):
        start = tile * LANES
        mixed = featured(channels + start) * featured(2 * channels + start)
        columns = pl.ds(pl.multiple_of(start, LANES), LANES)
        direct[:, columns] = skip[pl.ds(tile, 1), :] * mixed
        even, odd = exchange(mixed[:half], mixed[half:])
        signal_out[2 * tile] = even
        signal_out[2 * tile + 1] = odd

    @pl.loop(1, chips)
    def _(off):
        tile = lax.rem(chip + off, chips)
        make_signal(tile)
        signal_copy(2 * tile, 2 * off).start()
        signal_copy(2 * tile + 1, 2 * off + 1).start()

    make_signal(chip)
    signal_copy(sibling, 0).start()
    own = pltpu.make_async_copy(signal_out.at[me], signal_in.at[me], signal_got.at[me])
    own.start()

    @pl.loop(0, chips)
    def _(tile):
        start = tile * LANES
        query[:, pl.ds(pl.multiple_of(start, LANES), LANES)] = featured(start)

    @pl.loop(1, chips)
    def _(off):
        slot = lax.rem(me + shards - 2 * off, shards)
        arrived(taps_in.at[slot], taps_got.at[slot])
        taps_pass(off).start()

    banks = taps.shape[1]
    own_bank = bank[pl.ds(chip, 1), :]
    lane = lax.broadcasted_iota(jnp.int32, (1, LANES), 1)
    in_half = (lane < LANES // 2).astype(jnp.int32)
    own_bank = jnp.where(in_half + core == 1, own_bank, turned(own_bank))
    own_bank = jnp.broadcast_to(own_bank, (banks, LANES))
    pick = (lax.broadcasted_iota(jnp.int32, (banks, LANES), 0) == own_bank).astype(F32)
    nothing = jnp.zeros_like(pick)
    pick = jnp.concatenate(
        [
            jnp.concatenate([pick, nothing], axis=1),
            jnp.concatenate([nothing, pick], axis=1),
        ],
        axis=0,
    ).astype(BF16)

    def taps_block(slot):
        chosen = jnp.dot(taps_in[slot], pick, preferred_element_type=F32).astype(BF16)
        high = [chosen[:half, :LANES], chosen[:half, LANES:]]
        low = [chosen[half:, :LANES], chosen[half:, LANES:]]
        return jnp.concatenate(high + low + high, axis=0)

    def transform(low_slot, block, spec):
        both = jnp.concatenate([block(low_slot), block(low_slot + 1)], axis=1)
        both = jnp.dot(forward[...], both, preferred_element_type=F32)
        spec[low_slot] = both[:, :LANES]
        spec[low_slot + 1] = both[:, LANES:]

    @pl.loop(0, chips)
    def _(off):
        source = lax.rem(chip + chips - off, chips)
        slot = 2 * source + 1 - core
        arrived(taps_in.at[slot], taps_got.at[slot])
        transform(2 * source, taps_block, taps_spec)

    sign = lax.broadcasted_iota(jnp.int32, (steps, LANES), 0)
    sign = (1 - 2 * lax.rem(sign, 2)).astype(F32)
    left = lax.broadcasted_iota(jnp.int32, (steps, LANES), 1) < LANES // 2
    zero = jnp.zeros((steps, LANES), F32)

    def window(slot, before):
        real, imag = taps_spec[slot, :steps], taps_spec[slot, steps:]
        if before is None:
            return real, imag
        return (
            real - sign * taps_spec[before, steps:],
            imag + sign * taps_spec[before, :steps],
        )

    real, imag = window(0, None)
    pairs[0, :steps] = jnp.where(left, zero, real)
    pairs[0, steps:] = jnp.where(left, zero, imag)
    next_real, next_imag = window(1, 0)
    pairs[1, :steps] = jnp.where(left, real, next_real)
    pairs[1, steps:] = jnp.where(left, imag, next_imag)

    @pl.loop(2, shards)
    def _(slot):
        real, imag = window(slot - 1, slot - 2)
        next_real, next_imag = window(slot, slot - 1)
        pairs[slot, :steps] = jnp.where(left, real, next_real)
        pairs[slot, steps:] = jnp.where(left, imag, next_imag)

    def signal_block(slot):
        packed = signal_in[slot]
        other = turned(packed)
        return stacked(
            jnp.concatenate(
                [jnp.where(left_lanes, packed, other), jnp.where(left_lanes, other, packed)],
                axis=0,
            )
        )

    @pl.loop(0, chips)
    def _(step):
        off = lax.rem(step + 1, chips)
        low_slot = 2 * lax.rem(chip + chips - off, chips)
        arrived(signal_in.at[low_slot], signal_got.at[low_slot])
        arrived(signal_in.at[low_slot + 1], signal_got.at[low_slot + 1])
        transform(low_slot, signal_block, signal_spec)

    def result_copy(target, index):
        return remote(
            result_out.at[target],
            result_in.at[me],
            result_sent.at[index],
            result_got.at[me],
            target,
        )

    def make_result(pair):
        def add(slot, sums):
            real, imag = sums
            other = 2 * pair + 1 - slot
            left_real, left_imag = signal_spec[slot, :steps], signal_spec[slot, steps:]
            right_real, right_imag = pairs[other, :steps], pairs[other, steps:]
            return (
                real + (left_real * right_real - left_imag * right_imag),
                imag + (left_real * right_imag + left_imag * right_real),
            )

        real, imag = lax.fori_loop(0, 2 * pair + 2, add, (zero, zero))
        product = stacked(jnp.concatenate([real, imag], axis=0))
        convolved = jnp.dot(inverse[...], product, preferred_element_type=F32)
        even, odd = exchange(convolved[:half], convolved[half:])
        result_out[2 * pair] = even
        result_out[2 * pair + 1] = odd

    @pl.loop(1, chips)
    def _(off):
        pair = lax.rem(chip + off, chips)
        make_result(pair)
        result_copy(2 * pair, 2 * off).start()
        result_copy(2 * pair + 1, 2 * off + 1).start()

    make_result(chip)
    result_copy(sibling, 0).start()
    own = pltpu.make_async_copy(result_out.at[me], result_in.at[me], result_got.at[me])
    own.start()

    @pl.loop(0, chips)
    def _(step):
        off = lax.rem(step + 1, chips)
        tile = lax.rem(chip + chips - off, chips)
        arrived(result_in.at[2 * tile], result_got.at[2 * tile])
        arrived(result_in.at[2 * tile + 1], result_got.at[2 * tile + 1])
        top, bottom = exchange(result_in[2 * tile], result_in[2 * tile + 1])
        convolved = jnp.concatenate([top, bottom], axis=0)
        columns = pl.ds(pl.multiple_of(tile * LANES, LANES), LANES)
        out[:, columns] = (query[:, columns] * (convolved + direct[:, columns])).astype(BF16)

    taps_pass(0).wait_send()
    signal_copy(sibling, 0).wait_send()
    result_copy(sibling, 0).wait_send()

    @pl.loop(1, chips)
    def _(off):
        taps_copy(off).wait_send()
        taps_pass(off).wait_send()
        tile = lax.rem(chip + off, chips)
        signal_copy(2 * tile, 2 * off).wait_send()
        signal_copy(2 * tile + 1, 2 * off + 1).wait_send()
        result_copy(2 * tile, 2 * off).wait_send()
        result_copy(2 * tile + 1, 2 * off + 1).wait_send()


def per_device_blocks(projected, short_filter, filter_taps, bank, skip):
    steps = projected.shape[0]
    shards = lax.axis_size("context")
    channels = skip.shape[0]
    half = steps // 2
    forward, inverse = block_tables(steps)
    packed = (shards, half, LANES)
    spectra = (shards, 2 * steps, LANES)
    return pl.pallas_call(
        functools.partial(kernel, shards),
        out_shape=jax.ShapeDtypeStruct((steps, channels), BF16),
        in_specs=[pl.BlockSpec(memory_space=pltpu.VMEM)] * 7,
        out_specs=pl.BlockSpec(memory_space=pltpu.VMEM),
        scratch_shapes=[
            pltpu.VMEM((16, 3 * channels), BF16),
            pltpu.VMEM(packed, F32),
            pltpu.VMEM(packed, F32),
            pltpu.VMEM((shards, steps, LANES), BF16),
            pltpu.VMEM((steps, channels), F32),
            pltpu.VMEM((steps, channels), F32),
            pltpu.VMEM(spectra, F32),
            pltpu.VMEM(spectra, F32),
            pltpu.VMEM(spectra, F32),
            pltpu.VMEM(packed, F32),
            pltpu.VMEM(packed, F32),
            pltpu.SemaphoreType.DMA((2,)),
            pltpu.SemaphoreType.DMA((shards,)),
            pltpu.SemaphoreType.DMA((shards,)),
            pltpu.SemaphoreType.DMA((shards // 2,)),
            pltpu.SemaphoreType.DMA((shards // 2,)),
            pltpu.SemaphoreType.DMA((shards,)),
            pltpu.SemaphoreType.DMA((shards,)),
            pltpu.SemaphoreType.DMA((shards,)),
        ],
        compiler_params=pltpu.CompilerParams(
            collective_id=0, has_side_effects=True, vmem_limit_bytes=40 * 1024 * 1024
        ),
    )(
        projected,
        short_filter,
        filter_taps,
        bank.reshape(channels // LANES, LANES),
        skip.reshape(channels // LANES, LANES),
        jnp.asarray(forward),
        jnp.asarray(inverse),
    )


def per_device(projected, short_filter, filter_taps, bank, skip):
    shards = lax.axis_size("context")
    half_tile = skip.shape[0] // shards == LANES // 2 and filter_taps.shape[1] == LANES // 2
    if half_tile and shards % 2 == 0 and projected.shape[0] % 32 == 0:
        return per_device_blocks(projected, short_filter, filter_taps, bank, skip)
    return per_device_spectral(projected, short_filter, filter_taps, bank, skip)


def solution(mesh):
    in_specs = (P(("groups", "context"), None), P(), P("context", None), P(), P())
    out_specs = P(("groups", "context"), None)
    return jax.shard_map(
        per_device, mesh=mesh, in_specs=in_specs, out_specs=out_specs, check_vma=False
    )
```

```python
import functools
import math

import jax
import jax.numpy as jnp
import ml_dtypes
import numpy as np
from jax import lax
from jax.experimental import pallas as pl
from jax.experimental.pallas import tpu as pltpu
from jax.sharding import PartitionSpec as P

HIGHEST = lax.Precision.HIGHEST


def from_partner(array, axis, distance):
    return lax.ppermute(array, axis, [(i, i ^ 1 << distance) for i in range(lax.axis_size(axis))])


def from_behind(array, axis, by):
    count = lax.axis_size(axis)
    pairs = [(i, i + by) for i in range(count) if 0 <= i + by < count]
    return lax.ppermute(array, axis, pairs)


def phases(numer, period, sign):
    angle = sign * 2.0 * math.pi / period * (numer % period).astype(jnp.float32)
    return (jnp.cos(angle), jnp.sin(angle))


def local_table(length, sign):
    places = jnp.arange(length, dtype=jnp.int32)
    return phases(places[:, None] * places[None, :], length, sign)


def rotate(real, imag, cosine, sine):
    return (real * cosine - imag * sine, real * sine + imag * cosine)


def complex_product(left_real, left_imag, right_real, right_imag):
    out_real = jnp.dot(left_real, right_real, precision=HIGHEST) - jnp.dot(
        left_imag, right_imag, precision=HIGHEST
    )
    out_imag = jnp.dot(left_real, right_imag, precision=HIGHEST) + jnp.dot(
        left_imag, right_real, precision=HIGHEST
    )
    return (out_real, out_imag)


def forward_transform(real, imag, length_total, shards, my_index):
    levels = shards.bit_length() - 1
    steps = real.shape[0]
    for level in range(levels - 1, -1, -1):
        span = 1 << level
        other_real, other_imag = from_partner((real, imag), "context", level)
        upper = my_index >> level & 1 == 1
        cosine, sine = phases(my_index % span, 2 * span, -1.0)
        turned_real, turned_imag = rotate(other_real - real, other_imag - imag, cosine, sine)
        real = jnp.where(upper, turned_real, real + other_real)
        imag = jnp.where(upper, turned_imag, imag + other_imag)
    frequency = jnp.zeros((), jnp.int32)
    for level in range(levels):
        frequency = frequency | (my_index >> level & 1) << levels - 1 - level
    position = jnp.arange(steps, dtype=jnp.int32)
    cosine, sine = phases(position * frequency, length_total, -1.0)
    real, imag = rotate(real, imag, cosine[:, None], sine[:, None])
    table_cos, table_sin = local_table(steps, -1.0)
    real, imag = complex_product(table_cos, table_sin, real, imag)
    return (real, imag, frequency)


def inverse_transform(real, imag, frequency, length_total, shards, my_index):
    levels = shards.bit_length() - 1
    steps = real.shape[0]
    table_cos, table_sin = local_table(steps, 1.0)
    real, imag = complex_product(table_cos / steps, table_sin / steps, real, imag)
    position = jnp.arange(steps, dtype=jnp.int32)
    cosine, sine = phases(position * frequency, length_total, 1.0)
    real, imag = rotate(real, imag, cosine[:, None], sine[:, None])
    for level in range(levels):
        span = 1 << level
        other_real, other_imag = from_partner((real, imag), "context", level)
        upper = my_index >> level & 1 == 1
        cosine, sine = phases(my_index % span, 2 * span, 1.0)
        mine_real, mine_imag = rotate(real, imag, cosine, sine)
        theirs_real, theirs_imag = rotate(other_real, other_imag, cosine, sine)
        real_next = jnp.where(upper, 0.5 * (other_real - mine_real), 0.5 * (real + theirs_real))
        imag_next = jnp.where(upper, 0.5 * (other_imag - mine_imag), 0.5 * (imag + theirs_imag))
        real, imag = (real_next, imag_next)
    return (real, imag)


def per_device_spectral(projected, short_filter, filter_taps, bank, skip):
    steps = projected.shape[0]
    shards = lax.axis_size("context")
    my_index = lax.axis_index("context")
    length_total = steps * shards
    channels = skip.shape[0]
    banks = filter_taps.shape[1]
    earlier = from_behind(projected[steps - 2 :], "context", 1)
    joined = jnp.concatenate([earlier, projected], axis=0)
    weights = short_filter.astype(jnp.float32)
    featured = weights[0] * joined[2:] + weights[1] * joined[1:-1] + weights[2] * joined[:-2]
    query = featured[:, :channels]
    key_part = featured[:, channels : 2 * channels]
    value_part = featured[:, 2 * channels :]
    mixed = key_part * value_part
    signal = jnp.concatenate([mixed, filter_taps], axis=1)
    position = my_index * steps + jnp.arange(steps, dtype=jnp.int32)
    cosine, sine = phases(position, 2 * length_total, -1.0)
    real = jnp.concatenate([signal, signal * cosine[:, None]], axis=1)
    imag = jnp.concatenate([jnp.zeros_like(signal), signal * sine[:, None]], axis=1)
    spec_real, spec_imag, frequency = forward_transform(real, imag, length_total, shards, my_index)
    width = channels + banks
    selector = (bank[None, :] == jnp.arange(banks, dtype=jnp.int32)[:, None]).astype(jnp.float32)
    real_parts = []
    imag_parts = []
    for branch in range(2):
        offset = branch * width
        data_real = spec_real[:, offset : offset + channels]
        data_imag = spec_imag[:, offset : offset + channels]
        filter_real = jnp.dot(
            spec_real[:, offset + channels : offset + width], selector, precision=HIGHEST
        )
        filter_imag = jnp.dot(
            spec_imag[:, offset + channels : offset + width], selector, precision=HIGHEST
        )
        real_parts.append(data_real * filter_real - data_imag * filter_imag)
        imag_parts.append(data_real * filter_imag + data_imag * filter_real)
    product_real = jnp.concatenate(real_parts, axis=1)
    product_imag = jnp.concatenate(imag_parts, axis=1)
    back_real, back_imag = inverse_transform(
        product_real, product_imag, frequency, length_total, shards, my_index
    )
    cos_back, sin_back = phases(position, 2 * length_total, 1.0)
    second = (
        back_real[:, channels:] * cos_back[:, None] - back_imag[:, channels:] * sin_back[:, None]
    )
    convolved = 0.5 * (back_real[:, :channels] + second)
    return (query * (convolved + skip * mixed)).astype(jnp.bfloat16)


LANES = 128
F32 = jnp.float32
LEVELS = 64.0
TOP = 32766.0
CODE_ROWS = 16
BF16 = jnp.bfloat16


def split_rows(table):
    high = table.astype(ml_dtypes.bfloat16)
    low = (table - high.astype(np.float64)).astype(ml_dtypes.bfloat16)
    return np.concatenate([high, high, low], axis=1)


def block_tables(steps):
    angle = np.pi / steps * (np.arange(steps)[:, None] + 0.5) * np.arange(steps)[None, :]
    forward = np.concatenate([np.cos(angle), -np.sin(angle)], axis=0)
    inverse = np.concatenate([np.cos(angle.T), -np.sin(angle.T)], axis=1) / steps
    return split_rows(forward), split_rows(inverse)


def stacked(values):
    high = values.astype(BF16)
    low = (values - high.astype(F32)).astype(BF16)
    return jnp.concatenate([high, low, high], axis=0)


def coded(values):
    peak = jnp.maximum(jnp.max(jnp.abs(values), axis=0, keepdims=True), 1e-30)
    level = jnp.ceil(jnp.log2(peak) * LEVELS)
    whole = jnp.round(values * (jnp.exp2(level * (-1.0 / LEVELS)) * TOP)).astype(jnp.int32)
    level = jnp.broadcast_to(level, (CODE_ROWS, LANES)).astype(jnp.int32)
    return jnp.concatenate([whole, level], axis=0).astype(jnp.int16)


def decoded(words):
    numbers = words.astype(jnp.int32).astype(F32)
    rows = numbers.shape[0] - CODE_ROWS
    return numbers[:rows] * (jnp.exp2(numbers[rows : rows + 1] * (1.0 / LEVELS)) * (1.0 / TOP))


def kernel(
    shards,
    projected_far,
    short_filter,
    taps_far,
    bank,
    skip,
    forward_far,
    inverse_far,
    out,
    projected,
    taps,
    forward,
    inverse,
    load_sem,
    halo,
    signal_out,
    signal_in,
    taps_in,
    query,
    direct,
    signal_spec,
    taps_spec,
    pairs,
    result_out,
    result_in,
    halo_sem,
    signal_sent,
    signal_got,
    taps_sent,
    taps_passed,
    taps_got,
    result_sent,
    result_got,
):
    me = lax.axis_index("context")
    load_taps = pltpu.make_async_copy(taps_far, taps, load_sem.at[0])
    load_projected = pltpu.make_async_copy(projected_far, projected, load_sem.at[1])
    load_forward = pltpu.make_async_copy(forward_far, forward, load_sem.at[2])
    load_inverse = pltpu.make_async_copy(inverse_far, inverse, load_sem.at[3])
    load_taps.start()
    load_projected.start()
    load_forward.start()
    load_inverse.start()
    steps = projected.shape[0]
    half = steps // 2
    channels = out.shape[1]
    chips = shards // 2
    chip = lax.div(me, 2)
    core = lax.rem(me, 2)
    sibling = me + 1 - 2 * core
    left_lanes = lax.broadcasted_iota(jnp.int32, (half, LANES), 1) < LANES // 2

    def remote(src, dst, sent, got, target):
        return pltpu.make_async_remote_copy(
            src_ref=src,
            dst_ref=dst,
            send_sem=sent,
            recv_sem=got,
            device_id={"context": target},
            device_id_type=pl.DeviceIdType.MESH,
        )

    def arrived(ref, got):
        pltpu.make_async_copy(ref, ref, got).wait()

    def turned(values):
        return pltpu.roll(values, LANES // 2, 1)

    def exchange(first, second):
        return (
            jnp.where(left_lanes, first, turned(second)),
            jnp.where(left_lanes, turned(first), second),
        )

    barrier = pltpu.get_barrier_semaphore()
    for off in range(1, shards):
        pl.semaphore_signal(
            barrier,
            inc=1,
            device_id={"context": lax.rem(me + off, shards)},
            device_id_type=pl.DeviceIdType.MESH,
        )
    load_taps.wait()
    values = jnp.transpose(taps[...])
    values = jnp.concatenate([values[:half, :], values[half:, :]], axis=1)
    high = values.astype(BF16)
    taps_in[me] = jnp.concatenate([high, (values - high.astype(F32)).astype(BF16)], axis=0)
    load_projected.wait()
    pl.semaphore_wait(barrier, shards - 1)

    behind = remote(
        projected.at[pl.ds(steps - 16, 16)],
        halo,
        halo_sem.at[0],
        halo_sem.at[1],
        lax.rem(me + 1, shards),
    )
    behind.start()

    def taps_copy(off):
        target = lax.rem(me + 2 * off, shards)
        return remote(taps_in.at[me], taps_in.at[me], taps_sent.at[off], taps_got.at[me], target)

    def taps_pass(off):
        slot = lax.rem(me + shards - 2 * off, shards)
        return remote(
            taps_in.at[slot], taps_in.at[slot], taps_passed.at[off], taps_got.at[slot], sibling
        )

    taps_pass(0).start()

    @pl.loop(1, chips)
    def _(off):
        taps_copy(off).start()

    behind.wait()
    row = lax.broadcasted_iota(jnp.int32, (steps, LANES), 0)

    def featured(start):
        columns = pl.ds(pl.multiple_of(start, LANES), LANES)
        values = projected[:, columns].astype(F32)
        earlier = halo[:, columns].astype(F32)
        earlier = jnp.where(me == 0, 0.0, earlier)
        weights = short_filter[:, columns].astype(F32)
        last = earlier[15:16]
        once = jnp.where(row == 0, last, pltpu.roll(values, 1, 0))
        twice = jnp.where(
            row == 0, earlier[14:15], jnp.where(row == 1, last, pltpu.roll(values, 2, 0))
        )
        return weights[0:1] * values + weights[1:2] * once + weights[2:3] * twice

    def signal_copy(target, index):
        return remote(
            signal_out.at[target],
            signal_in.at[me],
            signal_sent.at[index],
            signal_got.at[me],
            target,
        )

    def make_signal(tile):
        start = tile * LANES
        mixed = featured(channels + start) * featured(2 * channels + start)
        columns = pl.ds(pl.multiple_of(start, LANES), LANES)
        direct[:, columns] = skip[pl.ds(tile, 1), :] * mixed
        even, odd = exchange(mixed[:half], mixed[half:])
        signal_out[2 * tile] = coded(even)
        signal_out[2 * tile + 1] = coded(odd)

    @pl.loop(1, chips)
    def _(off):
        tile = lax.rem(chip + off, chips)
        make_signal(tile)
        signal_copy(2 * tile, 2 * off).start()
        signal_copy(2 * tile + 1, 2 * off + 1).start()

    make_signal(chip)
    signal_copy(sibling, 0).start()
    own = pltpu.make_async_copy(signal_out.at[me], signal_in.at[me], signal_got.at[me])
    own.start()

    @pl.loop(0, chips)
    def _(tile):
        start = tile * LANES
        query[:, pl.ds(pl.multiple_of(start, LANES), LANES)] = featured(start)

    @pl.loop(1, chips)
    def _(off):
        slot = lax.rem(me + shards - 2 * off, shards)
        arrived(taps_in.at[slot], taps_got.at[slot])
        taps_pass(off).start()

    banks = taps.shape[0]
    own_bank = bank[pl.ds(chip, 1), :]
    lane = lax.broadcasted_iota(jnp.int32, (1, LANES), 1)
    in_half = (lane < LANES // 2).astype(jnp.int32)
    own_bank = jnp.where(in_half + core == 1, own_bank, turned(own_bank))
    own_bank = jnp.broadcast_to(own_bank, (banks, LANES))
    pick = (lax.broadcasted_iota(jnp.int32, (banks, LANES), 0) == own_bank).astype(F32)
    nothing = jnp.zeros_like(pick)
    pick = jnp.concatenate(
        [
            jnp.concatenate([pick, nothing], axis=1),
            jnp.concatenate([nothing, pick], axis=1),
        ],
        axis=0,
    ).astype(BF16)

    load_forward.wait()
    load_inverse.wait()

    def taps_block(slot):
        chosen = jnp.dot(taps_in[slot], pick, preferred_element_type=F32).astype(BF16)
        high = [chosen[:half, :LANES], chosen[:half, LANES:]]
        low = [chosen[half:, :LANES], chosen[half:, LANES:]]
        return jnp.concatenate(high + low + high, axis=0)

    def transform(low_slot, block, spec):
        both = jnp.concatenate([block(low_slot), block(low_slot + 1)], axis=1)
        both = jnp.dot(forward[...], both, preferred_element_type=F32)
        spec[low_slot] = both[:, :LANES]
        spec[low_slot + 1] = both[:, LANES:]

    @pl.loop(0, chips)
    def _(off):
        source = lax.rem(chip + chips - off, chips)
        slot = 2 * source + 1 - core
        arrived(taps_in.at[slot], taps_got.at[slot])
        transform(2 * source, taps_block, taps_spec)

    sign = lax.broadcasted_iota(jnp.int32, (steps, LANES), 0)
    sign = (1 - 2 * lax.rem(sign, 2)).astype(F32)
    left = lax.broadcasted_iota(jnp.int32, (steps, LANES), 1) < LANES // 2
    zero = jnp.zeros((steps, LANES), F32)

    def window(slot, before):
        real, imag = taps_spec[slot, :steps], taps_spec[slot, steps:]
        if before is None:
            return real, imag
        return (
            real - sign * taps_spec[before, steps:],
            imag + sign * taps_spec[before, :steps],
        )

    real, imag = window(0, None)
    pairs[0, :steps] = jnp.where(left, zero, real)
    pairs[0, steps:] = jnp.where(left, zero, imag)
    next_real, next_imag = window(1, 0)
    pairs[1, :steps] = jnp.where(left, real, next_real)
    pairs[1, steps:] = jnp.where(left, imag, next_imag)

    @pl.loop(2, shards)
    def _(slot):
        real, imag = window(slot - 1, slot - 2)
        next_real, next_imag = window(slot, slot - 1)
        pairs[slot, :steps] = jnp.where(left, real, next_real)
        pairs[slot, steps:] = jnp.where(left, imag, next_imag)

    def signal_block(slot):
        packed = decoded(signal_in[slot])
        other = turned(packed)
        return stacked(
            jnp.concatenate(
                [jnp.where(left_lanes, packed, other), jnp.where(left_lanes, other, packed)],
                axis=0,
            )
        )

    @pl.loop(0, chips)
    def _(step):
        off = lax.rem(step + 1, chips)
        low_slot = 2 * lax.rem(chip + chips - off, chips)
        arrived(signal_in.at[low_slot], signal_got.at[low_slot])
        arrived(signal_in.at[low_slot + 1], signal_got.at[low_slot + 1])
        transform(low_slot, signal_block, signal_spec)

    def result_copy(target, index):
        return remote(
            result_out.at[target],
            result_in.at[me],
            result_sent.at[index],
            result_got.at[me],
            target,
        )

    def make_result(pair):
        def add(slot, sums):
            real, imag = sums
            other = 2 * pair + 1 - slot
            left_real, left_imag = signal_spec[slot, :steps], signal_spec[slot, steps:]
            right_real, right_imag = pairs[other, :steps], pairs[other, steps:]
            return (
                real + (left_real * right_real - left_imag * right_imag),
                imag + (left_real * right_imag + left_imag * right_real),
            )

        real, imag = lax.fori_loop(0, 2 * pair + 2, add, (zero, zero))
        product = stacked(jnp.concatenate([real, imag], axis=0))
        convolved = jnp.dot(inverse[...], product, preferred_element_type=F32)
        even, odd = exchange(convolved[:half], convolved[half:])
        result_out[2 * pair] = coded(even)
        result_out[2 * pair + 1] = coded(odd)

    @pl.loop(1, chips)
    def _(off):
        pair = lax.rem(chip + off, chips)
        make_result(pair)
        result_copy(2 * pair, 2 * off).start()
        result_copy(2 * pair + 1, 2 * off + 1).start()

    make_result(chip)
    result_copy(sibling, 0).start()
    own = pltpu.make_async_copy(result_out.at[me], result_in.at[me], result_got.at[me])
    own.start()

    @pl.loop(0, chips)
    def _(step):
        off = lax.rem(step + 1, chips)
        tile = lax.rem(chip + chips - off, chips)
        arrived(result_in.at[2 * tile], result_got.at[2 * tile])
        arrived(result_in.at[2 * tile + 1], result_got.at[2 * tile + 1])
        top, bottom = exchange(
            decoded(result_in[2 * tile]), decoded(result_in[2 * tile + 1])
        )
        convolved = jnp.concatenate([top, bottom], axis=0)
        columns = pl.ds(pl.multiple_of(tile * LANES, LANES), LANES)
        out[:, columns] = (query[:, columns] * (convolved + direct[:, columns])).astype(BF16)

    taps_pass(0).wait_send()
    signal_copy(sibling, 0).wait_send()
    result_copy(sibling, 0).wait_send()

    @pl.loop(1, chips)
    def _(off):
        taps_copy(off).wait_send()
        taps_pass(off).wait_send()
        tile = lax.rem(chip + off, chips)
        signal_copy(2 * tile, 2 * off).wait_send()
        signal_copy(2 * tile + 1, 2 * off + 1).wait_send()
        result_copy(2 * tile, 2 * off).wait_send()
        result_copy(2 * tile + 1, 2 * off + 1).wait_send()


def per_device_blocks(projected, short_filter, filter_taps, bank, skip):
    steps = projected.shape[0]
    shards = lax.axis_size("context")
    channels = skip.shape[0]
    half = steps // 2
    forward, inverse = block_tables(steps)
    near = pl.BlockSpec(memory_space=pltpu.VMEM)
    far = pl.BlockSpec(memory_space=pltpu.HBM)
    packed = (shards, half + CODE_ROWS, LANES)
    spectra = (shards, 2 * steps, LANES)
    return pl.pallas_call(
        functools.partial(kernel, shards),
        out_shape=jax.ShapeDtypeStruct((steps, channels), BF16),
        in_specs=[far, near, far, near, near, far, far],
        out_specs=pl.BlockSpec(memory_space=pltpu.VMEM),
        scratch_shapes=[
            pltpu.VMEM(projected.shape, BF16),
            pltpu.VMEM(filter_taps.shape[::-1], F32),
            pltpu.VMEM(forward.shape, BF16),
            pltpu.VMEM(inverse.shape, BF16),
            pltpu.SemaphoreType.DMA((4,)),
            pltpu.VMEM((16, 3 * channels), BF16),
            pltpu.VMEM(packed, jnp.int16),
            pltpu.VMEM(packed, jnp.int16),
            pltpu.VMEM((shards, steps, LANES), BF16),
            pltpu.VMEM((steps, channels), F32),
            pltpu.VMEM((steps, channels), F32),
            pltpu.VMEM(spectra, F32),
            pltpu.VMEM(spectra, F32),
            pltpu.VMEM(spectra, F32),
            pltpu.VMEM(packed, jnp.int16),
            pltpu.VMEM(packed, jnp.int16),
            pltpu.SemaphoreType.DMA((2,)),
            pltpu.SemaphoreType.DMA((shards,)),
            pltpu.SemaphoreType.DMA((shards,)),
            pltpu.SemaphoreType.DMA((shards // 2,)),
            pltpu.SemaphoreType.DMA((shards // 2,)),
            pltpu.SemaphoreType.DMA((shards,)),
            pltpu.SemaphoreType.DMA((shards,)),
            pltpu.SemaphoreType.DMA((shards,)),
        ],
        compiler_params=pltpu.CompilerParams(
            collective_id=0, has_side_effects=True, vmem_limit_bytes=40 * 1024 * 1024
        ),
    )(
        projected,
        short_filter,
        filter_taps.T,
        bank.reshape(channels // LANES, LANES),
        skip.reshape(channels // LANES, LANES),
        jnp.asarray(forward),
        jnp.asarray(inverse),
    )


def per_device(projected, short_filter, filter_taps, bank, skip):
    shards = lax.axis_size("context")
    half_tile = skip.shape[0] // shards == LANES // 2 and filter_taps.shape[1] == LANES // 2
    if half_tile and shards % 2 == 0 and projected.shape[0] % 32 == 0:
        return per_device_blocks(projected, short_filter, filter_taps, bank, skip)
    return per_device_spectral(projected, short_filter, filter_taps, bank, skip)


def solution(mesh):
    in_specs = (P(("groups", "context"), None), P(), P("context", None), P(), P())
    out_specs = P(("groups", "context"), None)
    return jax.shard_map(
        per_device, mesh=mesh, in_specs=in_specs, out_specs=out_specs, check_vma=False
    )
```

```python
import functools
import math

import jax
import jax.numpy as jnp
import ml_dtypes
import numpy as np
from jax import lax
from jax.experimental import pallas as pl
from jax.experimental.pallas import tpu as pltpu
from jax.sharding import PartitionSpec as P

HIGHEST = lax.Precision.HIGHEST


def from_partner(array, axis, distance):
    return lax.ppermute(array, axis, [(i, i ^ 1 << distance) for i in range(lax.axis_size(axis))])


def from_behind(array, axis, by):
    count = lax.axis_size(axis)
    pairs = [(i, i + by) for i in range(count) if 0 <= i + by < count]
    return lax.ppermute(array, axis, pairs)


def phases(numer, period, sign):
    angle = sign * 2.0 * math.pi / period * (numer % period).astype(jnp.float32)
    return (jnp.cos(angle), jnp.sin(angle))


def local_table(length, sign):
    places = jnp.arange(length, dtype=jnp.int32)
    return phases(places[:, None] * places[None, :], length, sign)


def rotate(real, imag, cosine, sine):
    return (real * cosine - imag * sine, real * sine + imag * cosine)


def complex_product(left_real, left_imag, right_real, right_imag):
    out_real = jnp.dot(left_real, right_real, precision=HIGHEST) - jnp.dot(
        left_imag, right_imag, precision=HIGHEST
    )
    out_imag = jnp.dot(left_real, right_imag, precision=HIGHEST) + jnp.dot(
        left_imag, right_real, precision=HIGHEST
    )
    return (out_real, out_imag)


def forward_transform(real, imag, length_total, shards, my_index):
    levels = shards.bit_length() - 1
    steps = real.shape[0]
    for level in range(levels - 1, -1, -1):
        span = 1 << level
        other_real, other_imag = from_partner((real, imag), "context", level)
        upper = my_index >> level & 1 == 1
        cosine, sine = phases(my_index % span, 2 * span, -1.0)
        turned_real, turned_imag = rotate(other_real - real, other_imag - imag, cosine, sine)
        real = jnp.where(upper, turned_real, real + other_real)
        imag = jnp.where(upper, turned_imag, imag + other_imag)
    frequency = jnp.zeros((), jnp.int32)
    for level in range(levels):
        frequency = frequency | (my_index >> level & 1) << levels - 1 - level
    position = jnp.arange(steps, dtype=jnp.int32)
    cosine, sine = phases(position * frequency, length_total, -1.0)
    real, imag = rotate(real, imag, cosine[:, None], sine[:, None])
    table_cos, table_sin = local_table(steps, -1.0)
    real, imag = complex_product(table_cos, table_sin, real, imag)
    return (real, imag, frequency)


def inverse_transform(real, imag, frequency, length_total, shards, my_index):
    levels = shards.bit_length() - 1
    steps = real.shape[0]
    table_cos, table_sin = local_table(steps, 1.0)
    real, imag = complex_product(table_cos / steps, table_sin / steps, real, imag)
    position = jnp.arange(steps, dtype=jnp.int32)
    cosine, sine = phases(position * frequency, length_total, 1.0)
    real, imag = rotate(real, imag, cosine[:, None], sine[:, None])
    for level in range(levels):
        span = 1 << level
        other_real, other_imag = from_partner((real, imag), "context", level)
        upper = my_index >> level & 1 == 1
        cosine, sine = phases(my_index % span, 2 * span, 1.0)
        mine_real, mine_imag = rotate(real, imag, cosine, sine)
        theirs_real, theirs_imag = rotate(other_real, other_imag, cosine, sine)
        real_next = jnp.where(upper, 0.5 * (other_real - mine_real), 0.5 * (real + theirs_real))
        imag_next = jnp.where(upper, 0.5 * (other_imag - mine_imag), 0.5 * (imag + theirs_imag))
        real, imag = (real_next, imag_next)
    return (real, imag)


def per_device_spectral(projected, short_filter, filter_taps, bank, skip):
    steps = projected.shape[0]
    shards = lax.axis_size("context")
    my_index = lax.axis_index("context")
    length_total = steps * shards
    channels = skip.shape[0]
    banks = filter_taps.shape[1]
    earlier = from_behind(projected[steps - 2 :], "context", 1)
    joined = jnp.concatenate([earlier, projected], axis=0)
    weights = short_filter.astype(jnp.float32)
    featured = weights[0] * joined[2:] + weights[1] * joined[1:-1] + weights[2] * joined[:-2]
    query = featured[:, :channels]
    key_part = featured[:, channels : 2 * channels]
    value_part = featured[:, 2 * channels :]
    mixed = key_part * value_part
    signal = jnp.concatenate([mixed, filter_taps], axis=1)
    position = my_index * steps + jnp.arange(steps, dtype=jnp.int32)
    cosine, sine = phases(position, 2 * length_total, -1.0)
    real = jnp.concatenate([signal, signal * cosine[:, None]], axis=1)
    imag = jnp.concatenate([jnp.zeros_like(signal), signal * sine[:, None]], axis=1)
    spec_real, spec_imag, frequency = forward_transform(real, imag, length_total, shards, my_index)
    width = channels + banks
    selector = (bank[None, :] == jnp.arange(banks, dtype=jnp.int32)[:, None]).astype(jnp.float32)
    real_parts = []
    imag_parts = []
    for branch in range(2):
        offset = branch * width
        data_real = spec_real[:, offset : offset + channels]
        data_imag = spec_imag[:, offset : offset + channels]
        filter_real = jnp.dot(
            spec_real[:, offset + channels : offset + width], selector, precision=HIGHEST
        )
        filter_imag = jnp.dot(
            spec_imag[:, offset + channels : offset + width], selector, precision=HIGHEST
        )
        real_parts.append(data_real * filter_real - data_imag * filter_imag)
        imag_parts.append(data_real * filter_imag + data_imag * filter_real)
    product_real = jnp.concatenate(real_parts, axis=1)
    product_imag = jnp.concatenate(imag_parts, axis=1)
    back_real, back_imag = inverse_transform(
        product_real, product_imag, frequency, length_total, shards, my_index
    )
    cos_back, sin_back = phases(position, 2 * length_total, 1.0)
    second = (
        back_real[:, channels:] * cos_back[:, None] - back_imag[:, channels:] * sin_back[:, None]
    )
    convolved = 0.5 * (back_real[:, :channels] + second)
    return (query * (convolved + skip * mixed)).astype(jnp.bfloat16)


LANES = 128
F32 = jnp.float32
LEVELS = 64.0
TOP = 32766.0
CODE_ROWS = 16
VMEM_BYTES = 63 * 1024 * 1024
BF16 = jnp.bfloat16


def split_rows(table):
    high = table.astype(ml_dtypes.bfloat16)
    low = (table - high.astype(np.float64)).astype(ml_dtypes.bfloat16)
    return np.concatenate([high, high, low], axis=1)


def block_tables(steps):
    angle = np.pi / steps * (np.arange(steps)[:, None] + 0.5) * np.arange(steps)[None, :]
    forward = np.concatenate([np.cos(angle), -np.sin(angle)], axis=0)
    inverse = np.concatenate([np.cos(angle.T), -np.sin(angle.T)], axis=1) / steps
    return split_rows(forward), split_rows(inverse)


def stacked(values):
    high = values.astype(BF16)
    low = (values - high.astype(F32)).astype(BF16)
    return jnp.concatenate([high, low, high], axis=0)


def coded(values):
    peak = jnp.maximum(jnp.max(jnp.abs(values), axis=0, keepdims=True), 1e-30)
    level = jnp.ceil(jnp.log2(peak) * LEVELS)
    whole = jnp.round(values * (jnp.exp2(level * (-1.0 / LEVELS)) * TOP)).astype(jnp.int32)
    level = jnp.broadcast_to(level, (CODE_ROWS, LANES)).astype(jnp.int32)
    return jnp.concatenate([whole, level], axis=0).astype(jnp.int16)


def decoded(words):
    numbers = words.astype(jnp.int32).astype(F32)
    rows = numbers.shape[0] - CODE_ROWS
    return numbers[:rows] * (jnp.exp2(numbers[rows : rows + 1] * (1.0 / LEVELS)) * (1.0 / TOP))


def kernel(
    shards,
    projected_far,
    short_filter_far,
    taps_far,
    bank_far,
    skip_far,
    forward_far,
    inverse_far,
    out,
    projected,
    short_filter,
    taps,
    bank,
    skip,
    forward,
    inverse,
    load_sem,
    halo,
    signal_out,
    signal_in,
    taps_in,
    query,
    direct,
    signal_spec,
    taps_spec,
    pairs,
    result_out,
    result_in,
    halo_sem,
    signal_sent,
    signal_got,
    taps_sent,
    taps_passed,
    taps_got,
    result_sent,
    result_got,
):
    me = lax.axis_index("context")
    far = (
        taps_far,
        projected_far,
        short_filter_far,
        skip_far,
        bank_far,
        forward_far,
        inverse_far,
    )
    near = (taps, projected, short_filter, skip, bank, forward, inverse)
    loads = [
        pltpu.make_async_copy(source, target, load_sem.at[number])
        for number, (source, target) in enumerate(zip(far, near))
    ]
    for load in loads:
        load.start()
    steps = projected.shape[0]
    half = steps // 2
    channels = out.shape[1]
    chips = shards // 2
    chip = lax.div(me, 2)
    core = lax.rem(me, 2)
    sibling = me + 1 - 2 * core
    left_lanes = lax.broadcasted_iota(jnp.int32, (half, LANES), 1) < LANES // 2

    def remote(src, dst, sent, got, target):
        return pltpu.make_async_remote_copy(
            src_ref=src,
            dst_ref=dst,
            send_sem=sent,
            recv_sem=got,
            device_id={"context": target},
            device_id_type=pl.DeviceIdType.MESH,
        )

    def arrived(ref, got):
        pltpu.make_async_copy(ref, ref, got).wait()

    def turned(values):
        return pltpu.roll(values, LANES // 2, 1)

    def exchange(first, second):
        return (
            jnp.where(left_lanes, first, turned(second)),
            jnp.where(left_lanes, turned(first), second),
        )

    barrier = pltpu.get_barrier_semaphore()
    for off in range(1, shards):
        pl.semaphore_signal(
            barrier,
            inc=1,
            device_id={"context": lax.rem(me + off, shards)},
            device_id_type=pl.DeviceIdType.MESH,
        )
    loads[0].wait()
    values = jnp.transpose(taps[...])
    values = jnp.concatenate([values[:half, :], values[half:, :]], axis=1)
    high = values.astype(BF16)
    taps_in[me] = jnp.concatenate([high, (values - high.astype(F32)).astype(BF16)], axis=0)
    for load in loads[1:4]:
        load.wait()
    pl.semaphore_wait(barrier, shards - 1)

    behind = remote(
        projected.at[pl.ds(steps - 16, 16)],
        halo,
        halo_sem.at[0],
        halo_sem.at[1],
        lax.rem(me + 1, shards),
    )
    behind.start()

    def taps_copy(off):
        target = lax.rem(me + 2 * off, shards)
        return remote(taps_in.at[me], taps_in.at[me], taps_sent.at[off], taps_got.at[me], target)

    def taps_pass(off):
        slot = lax.rem(me + shards - 2 * off, shards)
        return remote(
            taps_in.at[slot], taps_in.at[slot], taps_passed.at[off], taps_got.at[slot], sibling
        )

    taps_pass(0).start()

    @pl.loop(1, chips)
    def _(off):
        taps_copy(off).start()

    behind.wait()
    row = lax.broadcasted_iota(jnp.int32, (steps, LANES), 0)

    def featured(start):
        columns = pl.ds(pl.multiple_of(start, LANES), LANES)
        values = projected[:, columns].astype(F32)
        earlier = halo[:, columns].astype(F32)
        earlier = jnp.where(me == 0, 0.0, earlier)
        weights = short_filter[:, columns].astype(F32)
        last = earlier[15:16]
        once = jnp.where(row == 0, last, pltpu.roll(values, 1, 0))
        twice = jnp.where(
            row == 0, earlier[14:15], jnp.where(row == 1, last, pltpu.roll(values, 2, 0))
        )
        return weights[0:1] * values + weights[1:2] * once + weights[2:3] * twice

    def signal_copy(target, index):
        return remote(
            signal_out.at[target],
            signal_in.at[me],
            signal_sent.at[index],
            signal_got.at[me],
            target,
        )

    def make_signal(tile):
        start = tile * LANES
        mixed = featured(channels + start) * featured(2 * channels + start)
        columns = pl.ds(pl.multiple_of(start, LANES), LANES)
        direct[:, columns] = skip[pl.ds(tile, 1), :] * mixed
        even, odd = exchange(mixed[:half], mixed[half:])
        signal_out[2 * tile] = coded(even)
        signal_out[2 * tile + 1] = coded(odd)

    @pl.loop(1, chips)
    def _(off):
        tile = lax.rem(chip + off, chips)
        make_signal(tile)
        signal_copy(2 * tile, 2 * off).start()
        signal_copy(2 * tile + 1, 2 * off + 1).start()

    make_signal(chip)
    signal_copy(sibling, 0).start()
    own = pltpu.make_async_copy(signal_out.at[me], signal_in.at[me], signal_got.at[me])
    own.start()

    @pl.loop(0, chips)
    def _(tile):
        start = tile * LANES
        query[:, pl.ds(pl.multiple_of(start, LANES), LANES)] = featured(start)

    @pl.loop(1, chips)
    def _(off):
        slot = lax.rem(me + shards - 2 * off, shards)
        arrived(taps_in.at[slot], taps_got.at[slot])
        taps_pass(off).start()

    for load in loads[4:]:
        load.wait()
    banks = taps.shape[0]
    own_bank = bank[pl.ds(chip, 1), :]
    lane = lax.broadcasted_iota(jnp.int32, (1, LANES), 1)
    in_half = (lane < LANES // 2).astype(jnp.int32)
    own_bank = jnp.where(in_half + core == 1, own_bank, turned(own_bank))
    own_bank = jnp.broadcast_to(own_bank, (banks, LANES))
    pick = (lax.broadcasted_iota(jnp.int32, (banks, LANES), 0) == own_bank).astype(F32)
    nothing = jnp.zeros_like(pick)
    pick = jnp.concatenate(
        [
            jnp.concatenate([pick, nothing], axis=1),
            jnp.concatenate([nothing, pick], axis=1),
        ],
        axis=0,
    ).astype(BF16)

    def taps_block(slot):
        chosen = jnp.dot(taps_in[slot], pick, preferred_element_type=F32).astype(BF16)
        high = [chosen[:half, :LANES], chosen[:half, LANES:]]
        low = [chosen[half:, :LANES], chosen[half:, LANES:]]
        return jnp.concatenate(high + low + high, axis=0)

    def transform(slots, block, spec):
        blocks = jnp.concatenate([block(slot) for slot in slots], axis=1)
        blocks = jnp.dot(forward[...], blocks, preferred_element_type=F32)
        for place, slot in enumerate(slots):
            spec[slot] = blocks[:, place * LANES : (place + 1) * LANES]

    def sources(first, count):
        found = []
        for off in range(first, min(first + count, chips)):
            found.append(lax.rem(chip + chips - off, chips))
        return found

    for first in range(0, chips, 4):
        slots = []
        for source in sources(first, 4):
            slot = 2 * source + 1 - core
            arrived(taps_in.at[slot], taps_got.at[slot])
            slots += [2 * source, 2 * source + 1]
        transform(slots, taps_block, taps_spec)

    sign = lax.broadcasted_iota(jnp.int32, (steps, LANES), 0)
    sign = (1 - 2 * lax.rem(sign, 2)).astype(F32)
    left = lax.broadcasted_iota(jnp.int32, (steps, LANES), 1) < LANES // 2
    zero = jnp.zeros((steps, LANES), F32)

    def window(slot, before):
        real, imag = taps_spec[slot, :steps], taps_spec[slot, steps:]
        if before is None:
            return real, imag
        return (
            real - sign * taps_spec[before, steps:],
            imag + sign * taps_spec[before, :steps],
        )

    real, imag = window(0, None)
    pairs[0, :steps] = jnp.where(left, zero, real)
    pairs[0, steps:] = jnp.where(left, zero, imag)
    next_real, next_imag = window(1, 0)
    pairs[1, :steps] = jnp.where(left, real, next_real)
    pairs[1, steps:] = jnp.where(left, imag, next_imag)

    @pl.loop(2, shards)
    def _(slot):
        real, imag = window(slot - 1, slot - 2)
        next_real, next_imag = window(slot, slot - 1)
        pairs[slot, :steps] = jnp.where(left, real, next_real)
        pairs[slot, steps:] = jnp.where(left, imag, next_imag)

    def signal_block(slot):
        packed = decoded(signal_in[slot])
        other = turned(packed)
        return stacked(
            jnp.concatenate(
                [jnp.where(left_lanes, packed, other), jnp.where(left_lanes, other, packed)],
                axis=0,
            )
        )

    for first in range(1, chips + 1, 2):
        slots = []
        for off in range(first, min(first + 2, chips + 1)):
            source = lax.rem(chip + chips - off, chips)
            slots += [2 * source, 2 * source + 1]
        for slot in slots:
            arrived(signal_in.at[slot], signal_got.at[slot])
        transform(slots, signal_block, signal_spec)

    def result_copy(target, index):
        return remote(
            result_out.at[target],
            result_in.at[me],
            result_sent.at[index],
            result_got.at[me],
            target,
        )

    def make_product(pair):
        def term(slot, real, imag):
            other = 2 * pair + 1 - slot
            left_real, left_imag = signal_spec[slot, :steps], signal_spec[slot, steps:]
            right_real, right_imag = pairs[other, :steps], pairs[other, steps:]
            return (
                real + (left_real * right_real - left_imag * right_imag),
                imag + (left_real * right_imag + left_imag * right_real),
            )

        def add(step, sums):
            return term(2 * step + 1, *term(2 * step, *sums))

        real, imag = lax.fori_loop(0, pair + 1, add, (zero, zero))
        return stacked(jnp.concatenate([real, imag], axis=0))

    for first in range(1, chips + 1, 2):
        offs = range(first, min(first + 2, chips + 1))
        made = [lax.rem(chip + off, chips) for off in offs]
        products = jnp.concatenate([make_product(pair) for pair in made], axis=1)
        convolved = jnp.dot(inverse[...], products, preferred_element_type=F32)
        for place, pair in enumerate(made):
            block = convolved[:, place * LANES : (place + 1) * LANES]
            even, odd = exchange(block[:half], block[half:])
            result_out[2 * pair] = coded(even)
            result_out[2 * pair + 1] = coded(odd)
        for off, pair in zip(offs, made):
            if off < chips:
                result_copy(2 * pair, 2 * off).start()
                result_copy(2 * pair + 1, 2 * off + 1).start()

    result_copy(sibling, 0).start()
    own = pltpu.make_async_copy(result_out.at[me], result_in.at[me], result_got.at[me])
    own.start()

    @pl.loop(0, chips)
    def _(step):
        off = lax.rem(step + 1, chips)
        tile = lax.rem(chip + chips - off, chips)
        arrived(result_in.at[2 * tile], result_got.at[2 * tile])
        arrived(result_in.at[2 * tile + 1], result_got.at[2 * tile + 1])
        top, bottom = exchange(
            decoded(result_in[2 * tile]), decoded(result_in[2 * tile + 1])
        )
        convolved = jnp.concatenate([top, bottom], axis=0)
        columns = pl.ds(pl.multiple_of(tile * LANES, LANES), LANES)
        out[:, columns] = (query[:, columns] * (convolved + direct[:, columns])).astype(BF16)

    taps_pass(0).wait_send()
    signal_copy(sibling, 0).wait_send()
    result_copy(sibling, 0).wait_send()

    @pl.loop(1, chips)
    def _(off):
        taps_copy(off).wait_send()
        taps_pass(off).wait_send()
        tile = lax.rem(chip + off, chips)
        signal_copy(2 * tile, 2 * off).wait_send()
        signal_copy(2 * tile + 1, 2 * off + 1).wait_send()
        result_copy(2 * tile, 2 * off).wait_send()
        result_copy(2 * tile + 1, 2 * off + 1).wait_send()


def per_device_blocks(projected, short_filter, filter_taps, bank, skip):
    steps = projected.shape[0]
    shards = lax.axis_size("context")
    channels = skip.shape[0]
    half = steps // 2
    forward, inverse = block_tables(steps)
    near = pl.BlockSpec(memory_space=pltpu.VMEM)
    far = pl.BlockSpec(memory_space=pl.ANY)
    tiles = (channels // LANES, LANES)
    packed = (shards, half + CODE_ROWS, LANES)
    spectra = (shards, 2 * steps, LANES)
    return pl.pallas_call(
        functools.partial(kernel, shards),
        out_shape=jax.ShapeDtypeStruct((steps, channels), BF16),
        in_specs=[far] * 7,
        out_specs=pl.BlockSpec(memory_space=pltpu.VMEM),
        scratch_shapes=[
            pltpu.VMEM(projected.shape, BF16),
            pltpu.VMEM(short_filter.shape, BF16),
            pltpu.VMEM(filter_taps.shape[::-1], F32),
            pltpu.VMEM(tiles, jnp.int32),
            pltpu.VMEM(tiles, F32),
            pltpu.VMEM(forward.shape, BF16),
            pltpu.VMEM(inverse.shape, BF16),
            pltpu.SemaphoreType.DMA((7,)),
            pltpu.VMEM((16, 3 * channels), BF16),
            pltpu.VMEM(packed, jnp.int16),
            pltpu.VMEM(packed, jnp.int16),
            pltpu.VMEM((shards, steps, LANES), BF16),
            pltpu.VMEM((steps, channels), F32),
            pltpu.VMEM((steps, channels), F32),
            pltpu.VMEM(spectra, F32),
            pltpu.VMEM(spectra, F32),
            pltpu.VMEM(spectra, F32),
            pltpu.VMEM(packed, jnp.int16),
            pltpu.VMEM(packed, jnp.int16),
            pltpu.SemaphoreType.DMA((2,)),
            pltpu.SemaphoreType.DMA((shards,)),
            pltpu.SemaphoreType.DMA((shards,)),
            pltpu.SemaphoreType.DMA((shards // 2,)),
            pltpu.SemaphoreType.DMA((shards // 2,)),
            pltpu.SemaphoreType.DMA((shards,)),
            pltpu.SemaphoreType.DMA((shards,)),
            pltpu.SemaphoreType.DMA((shards,)),
        ],
        compiler_params=pltpu.CompilerParams(
            collective_id=0, has_side_effects=True, vmem_limit_bytes=VMEM_BYTES
        ),
    )(
        projected,
        short_filter,
        filter_taps.T,
        bank.reshape(channels // LANES, LANES),
        skip.reshape(channels // LANES, LANES),
        jnp.asarray(forward),
        jnp.asarray(inverse),
    )


def per_device(projected, short_filter, filter_taps, bank, skip):
    shards = lax.axis_size("context")
    half_tile = skip.shape[0] // shards == LANES // 2 and filter_taps.shape[1] == LANES // 2
    if half_tile and shards % 2 == 0 and projected.shape[0] % 32 == 0:
        return per_device_blocks(projected, short_filter, filter_taps, bank, skip)
    return per_device_spectral(projected, short_filter, filter_taps, bank, skip)


def solution(mesh):
    in_specs = (P(("groups", "context"), None), P(), P("context", None), P(), P())
    out_specs = P(("groups", "context"), None)
    return jax.shard_map(
        per_device, mesh=mesh, in_specs=in_specs, out_specs=out_specs, check_vma=False
    )
```

```python
import functools
import math

import jax
import jax.numpy as jnp
import ml_dtypes
import numpy as np
from jax import lax
from jax.experimental import pallas as pl
from jax.experimental.pallas import tpu as pltpu
from jax.sharding import PartitionSpec as P

HIGHEST = lax.Precision.HIGHEST


def from_partner(array, axis, distance):
    return lax.ppermute(array, axis, [(i, i ^ 1 << distance) for i in range(lax.axis_size(axis))])


def from_behind(array, axis, by):
    count = lax.axis_size(axis)
    pairs = [(i, i + by) for i in range(count) if 0 <= i + by < count]
    return lax.ppermute(array, axis, pairs)


def phases(numer, period, sign):
    angle = sign * 2.0 * math.pi / period * (numer % period).astype(jnp.float32)
    return (jnp.cos(angle), jnp.sin(angle))


def local_table(length, sign):
    places = jnp.arange(length, dtype=jnp.int32)
    return phases(places[:, None] * places[None, :], length, sign)


def rotate(real, imag, cosine, sine):
    return (real * cosine - imag * sine, real * sine + imag * cosine)


def complex_product(left_real, left_imag, right_real, right_imag):
    out_real = jnp.dot(left_real, right_real, precision=HIGHEST) - jnp.dot(
        left_imag, right_imag, precision=HIGHEST
    )
    out_imag = jnp.dot(left_real, right_imag, precision=HIGHEST) + jnp.dot(
        left_imag, right_real, precision=HIGHEST
    )
    return (out_real, out_imag)


def forward_transform(real, imag, length_total, shards, my_index):
    levels = shards.bit_length() - 1
    steps = real.shape[0]
    for level in range(levels - 1, -1, -1):
        span = 1 << level
        other_real, other_imag = from_partner((real, imag), "context", level)
        upper = my_index >> level & 1 == 1
        cosine, sine = phases(my_index % span, 2 * span, -1.0)
        turned_real, turned_imag = rotate(other_real - real, other_imag - imag, cosine, sine)
        real = jnp.where(upper, turned_real, real + other_real)
        imag = jnp.where(upper, turned_imag, imag + other_imag)
    frequency = jnp.zeros((), jnp.int32)
    for level in range(levels):
        frequency = frequency | (my_index >> level & 1) << levels - 1 - level
    position = jnp.arange(steps, dtype=jnp.int32)
    cosine, sine = phases(position * frequency, length_total, -1.0)
    real, imag = rotate(real, imag, cosine[:, None], sine[:, None])
    table_cos, table_sin = local_table(steps, -1.0)
    real, imag = complex_product(table_cos, table_sin, real, imag)
    return (real, imag, frequency)


def inverse_transform(real, imag, frequency, length_total, shards, my_index):
    levels = shards.bit_length() - 1
    steps = real.shape[0]
    table_cos, table_sin = local_table(steps, 1.0)
    real, imag = complex_product(table_cos / steps, table_sin / steps, real, imag)
    position = jnp.arange(steps, dtype=jnp.int32)
    cosine, sine = phases(position * frequency, length_total, 1.0)
    real, imag = rotate(real, imag, cosine[:, None], sine[:, None])
    for level in range(levels):
        span = 1 << level
        other_real, other_imag = from_partner((real, imag), "context", level)
        upper = my_index >> level & 1 == 1
        cosine, sine = phases(my_index % span, 2 * span, 1.0)
        mine_real, mine_imag = rotate(real, imag, cosine, sine)
        theirs_real, theirs_imag = rotate(other_real, other_imag, cosine, sine)
        real_next = jnp.where(upper, 0.5 * (other_real - mine_real), 0.5 * (real + theirs_real))
        imag_next = jnp.where(upper, 0.5 * (other_imag - mine_imag), 0.5 * (imag + theirs_imag))
        real, imag = (real_next, imag_next)
    return (real, imag)


def per_device_spectral(projected, short_filter, filter_taps, bank, skip):
    steps = projected.shape[0]
    shards = lax.axis_size("context")
    my_index = lax.axis_index("context")
    length_total = steps * shards
    channels = skip.shape[0]
    banks = filter_taps.shape[1]
    earlier = from_behind(projected[steps - 2 :], "context", 1)
    joined = jnp.concatenate([earlier, projected], axis=0)
    weights = short_filter.astype(jnp.float32)
    featured = weights[0] * joined[2:] + weights[1] * joined[1:-1] + weights[2] * joined[:-2]
    query = featured[:, :channels]
    key_part = featured[:, channels : 2 * channels]
    value_part = featured[:, 2 * channels :]
    mixed = key_part * value_part
    signal = jnp.concatenate([mixed, filter_taps], axis=1)
    position = my_index * steps + jnp.arange(steps, dtype=jnp.int32)
    cosine, sine = phases(position, 2 * length_total, -1.0)
    real = jnp.concatenate([signal, signal * cosine[:, None]], axis=1)
    imag = jnp.concatenate([jnp.zeros_like(signal), signal * sine[:, None]], axis=1)
    spec_real, spec_imag, frequency = forward_transform(real, imag, length_total, shards, my_index)
    width = channels + banks
    selector = (bank[None, :] == jnp.arange(banks, dtype=jnp.int32)[:, None]).astype(jnp.float32)
    real_parts = []
    imag_parts = []
    for branch in range(2):
        offset = branch * width
        data_real = spec_real[:, offset : offset + channels]
        data_imag = spec_imag[:, offset : offset + channels]
        filter_real = jnp.dot(
            spec_real[:, offset + channels : offset + width], selector, precision=HIGHEST
        )
        filter_imag = jnp.dot(
            spec_imag[:, offset + channels : offset + width], selector, precision=HIGHEST
        )
        real_parts.append(data_real * filter_real - data_imag * filter_imag)
        imag_parts.append(data_real * filter_imag + data_imag * filter_real)
    product_real = jnp.concatenate(real_parts, axis=1)
    product_imag = jnp.concatenate(imag_parts, axis=1)
    back_real, back_imag = inverse_transform(
        product_real, product_imag, frequency, length_total, shards, my_index
    )
    cos_back, sin_back = phases(position, 2 * length_total, 1.0)
    second = (
        back_real[:, channels:] * cos_back[:, None] - back_imag[:, channels:] * sin_back[:, None]
    )
    convolved = 0.5 * (back_real[:, :channels] + second)
    return (query * (convolved + skip * mixed)).astype(jnp.bfloat16)


LANES = 128
F32 = jnp.float32
LEVELS = 64.0
TOP = 32766.0
CODE_ROWS = 16
VMEM_BYTES = 63 * 1024 * 1024
BF16 = jnp.bfloat16


def split_rows(table):
    high = table.astype(ml_dtypes.bfloat16)
    low = (table - high.astype(np.float64)).astype(ml_dtypes.bfloat16)
    return np.concatenate([high, high, low], axis=1)


def block_tables(steps):
    angle = np.pi / steps * (np.arange(steps)[:, None] + 0.5) * np.arange(steps)[None, :]
    forward = np.concatenate([np.cos(angle), -np.sin(angle)], axis=0)
    inverse = np.concatenate([np.cos(angle.T), -np.sin(angle.T)], axis=1) / steps
    return split_rows(forward), split_rows(inverse)


def stacked(values):
    high = values.astype(BF16)
    low = (values - high.astype(F32)).astype(BF16)
    return jnp.concatenate([high, low, high], axis=0)


def coded(values):
    peak = jnp.maximum(jnp.max(jnp.abs(values), axis=0, keepdims=True), 1e-30)
    level = jnp.ceil(jnp.log2(peak) * LEVELS)
    whole = jnp.round(values * (jnp.exp2(level * (-1.0 / LEVELS)) * TOP)).astype(jnp.int32)
    level = jnp.broadcast_to(level, (CODE_ROWS, LANES)).astype(jnp.int32)
    return jnp.concatenate([whole, level], axis=0).astype(jnp.int16)


def decoded(words):
    numbers = words.astype(jnp.int32).astype(F32)
    rows = numbers.shape[0] - CODE_ROWS
    return numbers[:rows] * (jnp.exp2(numbers[rows : rows + 1] * (1.0 / LEVELS)) * (1.0 / TOP))


def kernel(
    shards,
    projected_far,
    short_filter_far,
    taps_far,
    bank_far,
    skip_far,
    forward_far,
    inverse_far,
    out,
    projected,
    short_filter,
    taps,
    bank,
    skip,
    forward,
    inverse,
    load_sem,
    halo,
    signal_out,
    signal_in,
    taps_in,
    query,
    direct,
    signal_spec,
    taps_spec,
    pairs,
    result_out,
    result_in,
    halo_sem,
    signal_sent,
    signal_got,
    taps_sent,
    taps_passed,
    taps_got,
    result_sent,
    result_got,
):
    me = lax.axis_index("context")
    far = (
        taps_far,
        projected_far,
        short_filter_far,
        skip_far,
        bank_far,
        forward_far,
        inverse_far,
    )
    near = (taps, projected, short_filter, skip, bank, forward, inverse)
    loads = [
        pltpu.make_async_copy(source, target, load_sem.at[number])
        for number, (source, target) in enumerate(zip(far, near))
    ]
    for load in loads:
        load.start()
    steps = projected.shape[0]
    half = steps // 2
    channels = out.shape[1]
    chips = shards // 2
    chip = lax.div(me, 2)
    core = lax.rem(me, 2)
    sibling = me + 1 - 2 * core
    left_lanes = lax.broadcasted_iota(jnp.int32, (half, LANES), 1) < LANES // 2

    def remote(src, dst, sent, got, target):
        return pltpu.make_async_remote_copy(
            src_ref=src,
            dst_ref=dst,
            send_sem=sent,
            recv_sem=got,
            device_id={"context": target},
            device_id_type=pl.DeviceIdType.MESH,
        )

    def arrived(ref, got):
        pltpu.make_async_copy(ref, ref, got).wait()

    def turned(values):
        return pltpu.roll(values, LANES // 2, 1)

    def exchange(first, second):
        return (
            jnp.where(left_lanes, first, turned(second)),
            jnp.where(left_lanes, turned(first), second),
        )

    barrier = pltpu.get_barrier_semaphore()
    for off in range(1, shards):
        pl.semaphore_signal(
            barrier,
            inc=1,
            device_id={"context": lax.rem(me + off, shards)},
            device_id_type=pl.DeviceIdType.MESH,
        )
    loads[0].wait()
    values = jnp.transpose(taps[...])
    values = jnp.concatenate([values[:half, :], values[half:, :]], axis=1)
    high = values.astype(BF16)
    taps_in[me] = jnp.concatenate([high, (values - high.astype(F32)).astype(BF16)], axis=0)
    for load in loads[1:4]:
        load.wait()
    pl.semaphore_wait(barrier, shards - 1)

    behind = remote(
        projected.at[pl.ds(steps - 16, 16)],
        halo,
        halo_sem.at[0],
        halo_sem.at[1],
        lax.rem(me + 1, shards),
    )
    behind.start()

    def taps_copy(off):
        target = lax.rem(me + 2 * off, shards)
        return remote(taps_in.at[me], taps_in.at[me], taps_sent.at[off], taps_got.at[me], target)

    def taps_pass(off):
        slot = lax.rem(me + shards - 2 * off, shards)
        return remote(
            taps_in.at[slot], taps_in.at[slot], taps_passed.at[off], taps_got.at[slot], sibling
        )

    taps_pass(0).start()

    @pl.loop(1, chips)
    def _(off):
        taps_copy(off).start()

    behind.wait()
    row = lax.broadcasted_iota(jnp.int32, (steps, LANES), 0)

    def featured(start):
        columns = pl.ds(pl.multiple_of(start, LANES), LANES)
        values = projected[:, columns].astype(F32)
        earlier = halo[:, columns].astype(F32)
        earlier = jnp.where(me == 0, 0.0, earlier)
        weights = short_filter[:, columns].astype(F32)
        last = earlier[15:16]
        once = jnp.where(row == 0, last, pltpu.roll(values, 1, 0))
        twice = jnp.where(
            row == 0, earlier[14:15], jnp.where(row == 1, last, pltpu.roll(values, 2, 0))
        )
        return weights[0:1] * values + weights[1:2] * once + weights[2:3] * twice

    def signal_copy(target, index):
        return remote(
            signal_out.at[target],
            signal_in.at[me],
            signal_sent.at[index],
            signal_got.at[me],
            target,
        )

    def make_signal(tile):
        start = tile * LANES
        mixed = featured(channels + start) * featured(2 * channels + start)
        columns = pl.ds(pl.multiple_of(start, LANES), LANES)
        direct[:, columns] = skip[pl.ds(tile, 1), :] * mixed
        even, odd = exchange(mixed[:half], mixed[half:])
        signal_out[2 * tile] = coded(even)
        signal_out[2 * tile + 1] = coded(odd)

    @pl.loop(1, chips, unroll=True)
    def _(off):
        tile = lax.rem(chip + off, chips)
        make_signal(tile)
        signal_copy(2 * tile, 2 * off).start()
        signal_copy(2 * tile + 1, 2 * off + 1).start()

    make_signal(chip)
    signal_copy(sibling, 0).start()
    own = pltpu.make_async_copy(signal_out.at[me], signal_in.at[me], signal_got.at[me])
    own.start()

    @pl.loop(0, chips, unroll=True)
    def _(tile):
        start = tile * LANES
        query[:, pl.ds(pl.multiple_of(start, LANES), LANES)] = featured(start)

    @pl.loop(1, chips)
    def _(off):
        slot = lax.rem(me + shards - 2 * off, shards)
        arrived(taps_in.at[slot], taps_got.at[slot])
        taps_pass(off).start()

    for load in loads[4:]:
        load.wait()
    banks = taps.shape[0]
    own_bank = bank[pl.ds(chip, 1), :]
    lane = lax.broadcasted_iota(jnp.int32, (1, LANES), 1)
    in_half = (lane < LANES // 2).astype(jnp.int32)
    own_bank = jnp.where(in_half + core == 1, own_bank, turned(own_bank))
    own_bank = jnp.broadcast_to(own_bank, (banks, LANES))
    pick = (lax.broadcasted_iota(jnp.int32, (banks, LANES), 0) == own_bank).astype(F32)
    nothing = jnp.zeros_like(pick)
    pick = jnp.concatenate(
        [
            jnp.concatenate([pick, nothing], axis=1),
            jnp.concatenate([nothing, pick], axis=1),
        ],
        axis=0,
    ).astype(BF16)

    def taps_block(slot):
        chosen = jnp.dot(taps_in[slot], pick, preferred_element_type=F32).astype(BF16)
        high = [chosen[:half, :LANES], chosen[:half, LANES:]]
        low = [chosen[half:, :LANES], chosen[half:, LANES:]]
        return jnp.concatenate(high + low + high, axis=0)

    def transform(slots, block, spec):
        blocks = jnp.concatenate([block(slot) for slot in slots], axis=1)
        blocks = jnp.dot(forward[...], blocks, preferred_element_type=F32)
        for place, slot in enumerate(slots):
            spec[slot] = blocks[:, place * LANES : (place + 1) * LANES]

    def sources(first, count):
        found = []
        for off in range(first, min(first + count, chips)):
            found.append(lax.rem(chip + chips - off, chips))
        return found

    for first in range(0, chips, 4):
        slots = []
        for source in sources(first, 4):
            slot = 2 * source + 1 - core
            arrived(taps_in.at[slot], taps_got.at[slot])
            slots += [2 * source, 2 * source + 1]
        transform(slots, taps_block, taps_spec)

    sign = lax.broadcasted_iota(jnp.int32, (steps, LANES), 0)
    sign = (1 - 2 * lax.rem(sign, 2)).astype(F32)
    left = lax.broadcasted_iota(jnp.int32, (steps, LANES), 1) < LANES // 2
    zero = jnp.zeros((steps, LANES), F32)

    def window(slot, before):
        real, imag = taps_spec[slot, :steps], taps_spec[slot, steps:]
        if before is None:
            return real, imag
        return (
            real - sign * taps_spec[before, steps:],
            imag + sign * taps_spec[before, :steps],
        )

    real, imag = window(0, None)
    pairs[0, :steps] = jnp.where(left, zero, real)
    pairs[0, steps:] = jnp.where(left, zero, imag)
    next_real, next_imag = window(1, 0)
    pairs[1, :steps] = jnp.where(left, real, next_real)
    pairs[1, steps:] = jnp.where(left, imag, next_imag)

    @pl.loop(2, shards, unroll=True)
    def _(slot):
        real, imag = window(slot - 1, slot - 2)
        next_real, next_imag = window(slot, slot - 1)
        pairs[slot, :steps] = jnp.where(left, real, next_real)
        pairs[slot, steps:] = jnp.where(left, imag, next_imag)

    def signal_block(slot):
        packed = decoded(signal_in[slot])
        other = turned(packed)
        return stacked(
            jnp.concatenate(
                [jnp.where(left_lanes, packed, other), jnp.where(left_lanes, other, packed)],
                axis=0,
            )
        )

    for first in range(1, chips + 1, 2):
        slots = []
        for off in range(first, min(first + 2, chips + 1)):
            source = lax.rem(chip + chips - off, chips)
            slots += [2 * source, 2 * source + 1]
        for slot in slots:
            arrived(signal_in.at[slot], signal_got.at[slot])
        transform(slots, signal_block, signal_spec)

    def result_copy(target, index):
        return remote(
            result_out.at[target],
            result_in.at[me],
            result_sent.at[index],
            result_got.at[me],
            target,
        )

    def make_product(pair):
        def term(slot, real, imag):
            other = 2 * pair + 1 - slot
            left_real, left_imag = signal_spec[slot, :steps], signal_spec[slot, steps:]
            right_real, right_imag = pairs[other, :steps], pairs[other, steps:]
            return (
                real + (left_real * right_real - left_imag * right_imag),
                imag + (left_real * right_imag + left_imag * right_real),
            )

        def add(step, sums):
            return term(2 * step + 1, *term(2 * step, *sums))

        real, imag = lax.fori_loop(0, pair + 1, add, (zero, zero))
        return stacked(jnp.concatenate([real, imag], axis=0))

    for first in range(1, chips + 1, 2):
        offs = range(first, min(first + 2, chips + 1))
        made = [lax.rem(chip + off, chips) for off in offs]
        products = jnp.concatenate([make_product(pair) for pair in made], axis=1)
        convolved = jnp.dot(inverse[...], products, preferred_element_type=F32)
        for place, pair in enumerate(made):
            block = convolved[:, place * LANES : (place + 1) * LANES]
            even, odd = exchange(block[:half], block[half:])
            result_out[2 * pair] = coded(even)
            result_out[2 * pair + 1] = coded(odd)
        for off, pair in zip(offs, made):
            if off < chips:
                result_copy(2 * pair, 2 * off).start()
                result_copy(2 * pair + 1, 2 * off + 1).start()

    result_copy(sibling, 0).start()
    own = pltpu.make_async_copy(result_out.at[me], result_in.at[me], result_got.at[me])
    own.start()

    @pl.loop(0, chips, unroll=True)
    def _(step):
        off = lax.rem(step + 1, chips)
        tile = lax.rem(chip + chips - off, chips)
        arrived(result_in.at[2 * tile], result_got.at[2 * tile])
        arrived(result_in.at[2 * tile + 1], result_got.at[2 * tile + 1])
        top, bottom = exchange(
            decoded(result_in[2 * tile]), decoded(result_in[2 * tile + 1])
        )
        convolved = jnp.concatenate([top, bottom], axis=0)
        columns = pl.ds(pl.multiple_of(tile * LANES, LANES), LANES)
        out[:, columns] = (query[:, columns] * (convolved + direct[:, columns])).astype(BF16)

    taps_pass(0).wait_send()
    signal_copy(sibling, 0).wait_send()
    result_copy(sibling, 0).wait_send()

    @pl.loop(1, chips)
    def _(off):
        taps_copy(off).wait_send()
        taps_pass(off).wait_send()
        tile = lax.rem(chip + off, chips)
        signal_copy(2 * tile, 2 * off).wait_send()
        signal_copy(2 * tile + 1, 2 * off + 1).wait_send()
        result_copy(2 * tile, 2 * off).wait_send()
        result_copy(2 * tile + 1, 2 * off + 1).wait_send()


def per_device_blocks(projected, short_filter, filter_taps, bank, skip):
    steps = projected.shape[0]
    shards = lax.axis_size("context")
    channels = skip.shape[0]
    half = steps // 2
    forward, inverse = block_tables(steps)
    near = pl.BlockSpec(memory_space=pltpu.VMEM)
    far = pl.BlockSpec(memory_space=pl.ANY)
    tiles = (channels // LANES, LANES)
    packed = (shards, half + CODE_ROWS, LANES)
    spectra = (shards, 2 * steps, LANES)
    return pl.pallas_call(
        functools.partial(kernel, shards),
        out_shape=jax.ShapeDtypeStruct((steps, channels), BF16),
        in_specs=[far] * 7,
        out_specs=pl.BlockSpec(memory_space=pltpu.VMEM),
        scratch_shapes=[
            pltpu.VMEM(projected.shape, BF16),
            pltpu.VMEM(short_filter.shape, BF16),
            pltpu.VMEM(filter_taps.shape[::-1], F32),
            pltpu.VMEM(tiles, jnp.int32),
            pltpu.VMEM(tiles, F32),
            pltpu.VMEM(forward.shape, BF16),
            pltpu.VMEM(inverse.shape, BF16),
            pltpu.SemaphoreType.DMA((7,)),
            pltpu.VMEM((16, 3 * channels), BF16),
            pltpu.VMEM(packed, jnp.int16),
            pltpu.VMEM(packed, jnp.int16),
            pltpu.VMEM((shards, steps, LANES), BF16),
            pltpu.VMEM((steps, channels), F32),
            pltpu.VMEM((steps, channels), F32),
            pltpu.VMEM(spectra, F32),
            pltpu.VMEM(spectra, F32),
            pltpu.VMEM(spectra, F32),
            pltpu.VMEM(packed, jnp.int16),
            pltpu.VMEM(packed, jnp.int16),
            pltpu.SemaphoreType.DMA((2,)),
            pltpu.SemaphoreType.DMA((shards,)),
            pltpu.SemaphoreType.DMA((shards,)),
            pltpu.SemaphoreType.DMA((shards // 2,)),
            pltpu.SemaphoreType.DMA((shards // 2,)),
            pltpu.SemaphoreType.DMA((shards,)),
            pltpu.SemaphoreType.DMA((shards,)),
            pltpu.SemaphoreType.DMA((shards,)),
        ],
        compiler_params=pltpu.CompilerParams(
            collective_id=0, has_side_effects=True, vmem_limit_bytes=VMEM_BYTES
        ),
    )(
        projected,
        short_filter,
        filter_taps.T,
        bank.reshape(channels // LANES, LANES),
        skip.reshape(channels // LANES, LANES),
        jnp.asarray(forward),
        jnp.asarray(inverse),
    )


def per_device(projected, short_filter, filter_taps, bank, skip):
    shards = lax.axis_size("context")
    half_tile = skip.shape[0] // shards == LANES // 2 and filter_taps.shape[1] == LANES // 2
    if half_tile and shards % 2 == 0 and projected.shape[0] % 32 == 0:
        return per_device_blocks(projected, short_filter, filter_taps, bank, skip)
    return per_device_spectral(projected, short_filter, filter_taps, bank, skip)


def solution(mesh):
    in_specs = (P(("groups", "context"), None), P(), P("context", None), P(), P())
    out_specs = P(("groups", "context"), None)
    return jax.shard_map(
        per_device, mesh=mesh, in_specs=in_specs, out_specs=out_specs, check_vma=False
    )
```
